32 devices in a mesh: band: 8 (over y, x, core), plane: 4 (over z).
Axes of the slice: x: 2, y: 2, z: 4, core: 2. Of those that a mesh axis runs over, the one named last changes fastest.
Arguments:
- orbitals: bfloat16 [64, 128, 128, 128], P('band', 'plane'), may hold values from -6 to 6
- potential_slots: bfloat16 [8, 2, 128, 128, 128], P('band', None, 'plane'), may hold values from -6 to 6
- pattern_owner: int32 [4], replicated, may hold values from 0 to 7, as said below
- retained: int32 [3, 64], replicated, may hold values from 0 to 127, as said below
- band_energy: float32 [64], P('band'), may hold values from 0.5 to 8
Outputs:
- rhs: float32 [64, 4, 64, 64, 128], P('band', None, None, 'plane')
The draws below stay inside these ranges and needn't reach their ends.
Inputs may be any that keep to these rules, and one draw needn't show every extreme that they name: pattern_owner holds 4 distinct slot indices. Each row of retained holds 64 distinct frequency indices.
All inputs are finite; a program needn't handle non-finite values.
Results may differ from the reference program's by a relative error of at most 0.0003.
Values may be sent and summed in bfloat16 or wider, within the bound.
No kernel may reach another device: no remote copies, remote signals or barrier semaphores. Data moves between devices by JAX's collectives and lax.ppermute only.
A program may use at most 192 MiB of HBM per device.

```python
import math
import jax
import jax.numpy as jnp
from jax import lax

NGRID = 128
KEEP = 64
NB = 64
NPERT = 4
N_BAND = 8


def distinct_with_ends(key, total, count):
    inner = jax.random.permutation(jax.random.fold_in(key, 3), total - 2)[:count - 2].astype(jnp.int32) + 1
    picked = jnp.concatenate([jnp.array([0, total - 1], dtype=jnp.int32), inner])
    order = jax.random.permutation(jax.random.fold_in(key, 5), count)
    return picked[order].astype(jnp.int32)


def draw_pattern_owner(key, part):
    return distinct_with_ends(jax.random.fold_in(key, 7), N_BAND, NPERT)


def draw_retained(key, part):
    chosen = [distinct_with_ends(jax.random.fold_in(key, 11 + dimension), NGRID, KEEP) for dimension in range(3)]
    return jnp.stack(chosen).astype(jnp.int32)


def level_of(key, dims, pieces, smallest, high):
    loudness, own = 1.0, jax.random.fold_in(key, 6)
    for axis_at, blocks in pieces:
        draws = jnp.exp(jax.random.uniform(jax.random.fold_in(own, axis_at), (blocks,), jnp.float32, smallest / len(pieces), high / len(pieces)))
        loudness = loudness * jnp.repeat(draws, dims[axis_at] // blocks).reshape([-1 if axis == axis_at else 1 for axis in range(len(dims))])
    return loudness


def scatter_about(own_key, shape, width, reach, shards=(), kind=jnp.bfloat16):
    values = width * jax.random.normal(own_key, shape, jnp.float32)
    if shards:
        values = values * level_of(own_key, shape, shards, -0.22, 0.18)
    return jnp.clip(values, -reach, reach).astype(kind)


def setup_inputs(seed: int = 0) -> dict:
    key_list = jax.random.split(jax.random.key(seed), 6)
    return {
        "orbitals": scatter_about(key_list[0], (NB, NGRID, NGRID, NGRID), 1.0, 6.0, ((0, 8), (1, 4))),
        "potential_slots": scatter_about(key_list[1], (N_BAND, 2, NGRID, NGRID, NGRID), 1.0, 6.0, ((0, 8), (2, 4))),
        "pattern_owner": draw_pattern_owner(jax.random.fold_in(key_list[5], 71), 0),
        "retained": draw_retained(jax.random.fold_in(key_list[5], 71), 0),
        "band_energy": jnp.clip(jnp.exp(math.log(8.0) - 2.7725887 * jax.random.uniform(key_list[4], (NB,), jnp.float32) ** level_of(key_list[4], (NB,), ((0, 8),), -0.2, 0.2)), 0.5, 8.0),
    }


kinetic_coef = 0.5 * (2.0 * math.pi / 64.0) ** 2

def freq_table(frequency, length):
    position = jnp.arange(length, dtype=jnp.int32)
    phase_index = position[:, None] * frequency[None, :].astype(jnp.int32) % length
    angles = phase_index.astype(jnp.float32) * (2.0 * math.pi / length)
    norm_factor = 1.0 / math.sqrt(length)
    return (jnp.cos(angles) * norm_factor, -jnp.sin(angles) * norm_factor)

def signed_square(frequency, length):
    signed = jnp.where(frequency < length // 2, frequency, frequency - length).astype(jnp.float32)
    return signed * signed

def complex_step(real_part, imag_part, cos_table, sin_table, einsum_form):
    highest = lax.Precision.HIGHEST
    out_real = jnp.einsum(einsum_form, real_part, cos_table, precision=highest) - jnp.einsum(einsum_form, imag_part, sin_table, precision=highest)
    out_imag = jnp.einsum(einsum_form, real_part, sin_table, precision=highest) + jnp.einsum(einsum_form, imag_part, cos_table, precision=highest)
    return (out_real, out_imag)

def reference(orbitals, potential_slots, pattern_owner, retained, band_energy):
    cos_x, sin_x = freq_table(retained[0], NGRID)
    cos_y, sin_y = freq_table(retained[1], NGRID)
    cos_z, sin_z = freq_table(retained[2], NGRID)
    kinetic = kinetic_coef * (signed_square(retained[0], NGRID)[:, None, None] + signed_square(retained[1], NGRID)[None, :, None] + signed_square(retained[2], NGRID)[None, None, :])
    potentials = jnp.take(potential_slots, pattern_owner, axis=0).astype(jnp.float32)

    def one_band(carry_in):
        orbital, energy = carry_in
        density = orbital.astype(jnp.float32)
        real_part = density[None] * potentials[:, 0]
        imag_part = density[None] * potentials[:, 1]
        real_part, imag_part = complex_step(real_part, imag_part, cos_z, sin_z, 'pxyz,zl->pxyl')
        real_part, imag_part = complex_step(real_part, imag_part, cos_y, sin_y, 'pxyl,yj->pxjl')
        real_part, imag_part = complex_step(real_part, imag_part, cos_x, sin_x, 'pxjl,xi->pijl')
        precond = 1.0 / (1.0 + kinetic / energy)
        return jnp.concatenate([real_part * precond[None], imag_part * precond[None]], axis=-1)
    return lax.map(one_band, (orbitals, band_energy))
```

```python
import functools
import math

import jax
import jax.numpy as jnp
from jax import lax
from jax.experimental import pallas as pl
from jax.experimental.pallas import tpu as pltpu
from jax.sharding import PartitionSpec as P

kinetic_coef = 0.5 * (2.0 * math.pi / 64.0) ** 2
code_top = 32700.0
code_steps = 256.0 / math.log(2.0)
vmem_limit = 56 * 1024 * 1024
f32 = jnp.float32
bf16 = jnp.bfloat16


def angle_table(frequency, position, length):
    phase_index = position[:, None] * frequency[None, :] % length
    angles = phase_index.astype(f32) * (2.0 * math.pi / length)
    norm_factor = 1.0 / math.sqrt(length)
    return jnp.cos(angles) * norm_factor, -jnp.sin(angles) * norm_factor


def signed_square(frequency, length):
    signed = jnp.where(frequency < length // 2, frequency, frequency - length).astype(f32)
    return signed * signed


def split_table(value):
    high = lax.reduce_precision(value, 8, 7)
    return high.astype(bf16), (value - high).astype(bf16)


def split_pair(value):
    high = value.astype(bf16)
    low = (value - high.astype(f32)).astype(bf16)
    return high, low


def left_table(frequency, position, length):
    cos, sin = angle_table(frequency, position, length)
    high, low = split_table(jnp.concatenate([cos, sin], axis=1).T)
    top = jnp.concatenate([high, high], axis=1)
    bottom = jnp.concatenate([low, jnp.zeros_like(low)], axis=1)
    return jnp.concatenate([top, bottom], axis=0)


def right_table(frequency, position, length):
    cos, sin = angle_table(frequency, position, length)
    table = jnp.concatenate(
        [jnp.concatenate([cos, sin], axis=1), jnp.concatenate([-sin, cos], axis=1)], axis=0
    )
    return jnp.concatenate(split_table(table), axis=1)


def left_dot(table, planes, keep):
    stacked = jnp.concatenate(
        [jnp.concatenate(split_pair(plane), axis=0) for plane in planes], axis=1
    )
    sums = jnp.dot(table, stacked, preferred_element_type=f32)
    half = 2 * keep
    sums = sums[:half] + sums[half:]
    lane = lax.broadcasted_iota(jnp.int32, (keep, half), 1)
    results = []
    for index in range(len(planes)):
        part = sums[:, index * half : (index + 1) * half]
        turned = pltpu.roll(part[keep:], keep, 1)
        results.append(part[:keep] + jnp.where(lane < keep, -turned, turned))
    return results


def forward_kernel(
    slots, planes_total, step_planes, keep, columns, patterns, parts,
    source_ref, target_ref, orbital_ref, wz_ref, ty_ref, *rest
):
    potential_refs = rest[:slots]
    out_refs = rest[slots : slots + parts]
    potential, held, semaphore = rest[slots + parts :]
    band, step = pl.program_id(0), pl.program_id(1)

    @pl.when((band == 0) & (step == 0))
    def _():
        def fetch(block, pattern):
            return pltpu.make_async_copy(block, potential.at[pattern], semaphore.at[pattern])

        gathered = slots == 1
        for pattern in range(patterns):
            if gathered:
                fetch(potential_refs[0].at[source_ref[pattern]], pattern).start()
            for slot in range(0 if gathered else slots):

                @pl.when(source_ref[pattern] == slot)
                def _():
                    fetch(potential_refs[slot], pattern).start()

        for pattern in range(patterns):
            fetch(potential_refs[0].at[0] if gathered else potential_refs[0], pattern).wait()

    def one_plane(index, carry):
        at = step * step_planes + index
        orbital = orbital_ref[0, index].astype(f32)
        highs, lows = [], []
        for pattern in range(patterns):
            split = [
                split_pair(orbital * potential[pattern, part, at].astype(f32)) for part in range(2)
            ]
            highs.append(jnp.concatenate([split[0][0], split[1][0]], axis=1))
            lows.append(jnp.concatenate([split[0][1], split[1][1]], axis=1))
        half = 2 * keep
        high_sum = jnp.dot(
            jnp.concatenate(highs, axis=0), wz_ref[...], preferred_element_type=f32
        )
        low_sum = jnp.dot(
            jnp.concatenate(lows, axis=0), wz_ref[:, :half], preferred_element_type=f32
        )
        along_z = high_sum[:, :half] + high_sum[:, half:] + low_sum
        length = orbital.shape[0]
        for pair in range(patterns // 2):
            first = 2 * pair
            results = left_dot(
                ty_ref[...],
                [along_z[p * length : (p + 1) * length] for p in (first, first + 1)],
                keep,
            )
            for offset, result in enumerate(results):
                for part in range(parts):
                    held[first + offset, at, part] = result[part * columns : (part + 1) * columns]
        return carry

    lax.fori_loop(0, step_planes, one_plane, 0, unroll=math.gcd(step_planes, 4))

    @pl.when(step == pl.num_programs(1) - 1)
    def _():
        rows = planes_total * columns
        for shift in range(parts):
            target = target_ref[shift]
            out_ref = out_refs[shift]
            for pair in range(patterns // 2):
                inverse = []
                for pattern in (2 * pair, 2 * pair + 1):
                    top = jnp.zeros((columns, 2 * keep), f32)
                    for at in range(planes_total):
                        top = jnp.maximum(top, jnp.abs(held[pattern, at, target]))
                    top = jnp.max(top, axis=0, keepdims=True)
                    code = jnp.ceil(
                        jnp.log(jnp.maximum(top, 1e-30) * (1.0 / code_top)) * code_steps
                    )
                    inverse.append(jnp.exp(code * (-1.0 / code_steps)))
                    row = (patterns // 2) * rows + pattern
                    out_ref[0, row : row + 1, :] = code.astype(jnp.int32)
                for at in range(planes_total):
                    low, high = [
                        jnp.round(held[2 * pair + which, at, target] * inverse[which]).astype(
                            jnp.int32
                        )
                        for which in range(2)
                    ]
                    row = pair * rows + at * columns
                    out_ref[0, row : row + columns, :] = (high << 16) | (low & 0xFFFF)


def forward(
    orbitals, potentials, source, targets, wz, ty, first_plane, planes, step_planes, first_band,
    bands, keep, patterns
):
    parts = targets.shape[0]
    columns = keep // parts
    length = orbitals.shape[2]
    slots = len(potentials)
    rows = (patterns // 2) * planes * columns + 8
    kernel = functools.partial(
        forward_kernel, slots, planes, step_planes, keep, columns, patterns, parts
    )
    whole = pl.BlockSpec(memory_space=pl.ANY)
    fixed = lambda array: pl.BlockSpec(array.shape, lambda b, g, *_: (0,) * array.ndim)
    flops = 16 * bands * planes * patterns * length * length * 2 * keep
    return pl.pallas_call(
        kernel,
        grid_spec=pltpu.PrefetchScalarGridSpec(
            num_scalar_prefetch=2,
            grid=(bands, planes // step_planes),
            in_specs=[
                pl.BlockSpec(
                    (1, step_planes, length, length),
                    lambda b, g, *_: (b + first_band, g + first_plane // step_planes, 0, 0),
                ),
                fixed(wz),
                fixed(ty),
            ]
            + [whole] * slots,
            out_specs=[pl.BlockSpec((1, rows, 2 * keep), lambda b, g, *_: (b, 0, 0))] * parts,
            scratch_shapes=[
                pltpu.VMEM((patterns, 2, planes, length, length), bf16),
                pltpu.VMEM((patterns, planes, parts, columns, 2 * keep), f32),
                pltpu.SemaphoreType.DMA((patterns,)),
            ],
        ),
        out_shape=[jax.ShapeDtypeStruct((bands, rows, 2 * keep), jnp.int32)] * parts,
        compiler_params=pltpu.CompilerParams(
            dimension_semantics=("arbitrary", "arbitrary"), vmem_limit_bytes=vmem_limit
        ),
        cost_estimate=pl.CostEstimate(
            flops=flops, bytes_accessed=2 * bands * planes * length * length, transcendentals=0
        ),
        name="forward_zy",
    )(source, targets, orbitals, wz, ty, *potentials)


def final_kernel(
    plane_counts, first_band, keep, columns, patterns, parts, chained,
    ky_ref, energy_ref, tx_ref, kinetic_ref, *rest
):
    count = len(plane_counts) * parts
    chunk_refs = rest[:count]
    out_ref, wide = rest[count + chained :]
    energy = energy_ref[pl.program_id(0) + first_band]
    total = parts * sum(plane_counts)
    for pair in range(patterns // 2):
        base = 0
        for chunk, planes in enumerate(plane_counts):
            rows = planes * columns
            for shift in range(parts):
                ref = chunk_refs[chunk * parts + shift]
                scales = []
                for pattern in (2 * pair, 2 * pair + 1):
                    row = (patterns // 2) * rows + pattern
                    scales.append(jnp.exp(ref[0, row : row + 1, :].astype(f32) * (1.0 / code_steps)))
                words = ref[0, pair * rows : (pair + 1) * rows, :]
                wide[0, base : base + rows, :] = ((words << 16) >> 16).astype(f32) * scales[0]
                wide[1, base : base + rows, :] = (words >> 16).astype(f32) * scales[1]
                base += rows

        def two_columns(index, carry):
            for which in range(2):
                column = [2 * index, 2 * index + 1]
                results = left_dot(
                    tx_ref[...],
                    [wide[which, pl.ds(j, total, stride=columns), :] for j in column],
                    keep,
                )
                for j, result in zip(column, results):
                    kinetic = kinetic_ref[...] + ky_ref[j]
                    out_ref[0, 2 * pair + which, pl.ds(j, keep, stride=columns), :] = (
                        result * (1.0 / (1.0 + kinetic / energy))
                    )
            return carry

        lax.fori_loop(0, columns // 2, two_columns, 0, unroll=math.gcd(columns // 2, 4))


def final(chunks, plane_counts, band_offsets, first_band, bands, held_out, ky, energy, tx, kinetic, patterns, keep, all_bands):
    parts = len(chunks[0])
    columns = keep // parts
    total = parts * sum(plane_counts)
    chained = 0 if held_out is None else 1
    kernel = functools.partial(
        final_kernel, plane_counts, first_band, keep, columns, patterns, parts, chained
    )
    fixed = lambda array: pl.BlockSpec(array.shape, lambda b, *_: (0,) * array.ndim)
    chunk_specs = []
    for arrays, offset in zip(chunks, band_offsets):
        for array in arrays:
            chunk_specs.append(
                pl.BlockSpec((1,) + array.shape[1:], lambda b, *_, o=offset: (b + o, 0, 0))
            )
    flat = [array for arrays in chunks for array in arrays]
    out_block = (1, patterns, keep * columns, 2 * keep)
    operands = [ky, energy, tx, kinetic] + flat
    if chained:
        operands.append(held_out)
    return pl.pallas_call(
        kernel,
        grid_spec=pltpu.PrefetchScalarGridSpec(
            num_scalar_prefetch=2,
            grid=(bands,),
            in_specs=[fixed(tx), fixed(kinetic)]
            + chunk_specs
            + [pl.BlockSpec(memory_space=pl.ANY)] * chained,
            out_specs=pl.BlockSpec(out_block, lambda b, *_: (b + first_band, 0, 0, 0)),
            scratch_shapes=[pltpu.VMEM((2, total * columns, 2 * keep), f32)],
        ),
        out_shape=jax.ShapeDtypeStruct((all_bands,) + out_block[1:], f32),
        input_output_aliases={len(operands) - 1: 0} if chained else {},
        compiler_params=pltpu.CompilerParams(
            dimension_semantics=("arbitrary",), vmem_limit_bytes=vmem_limit
        ),
        cost_estimate=pl.CostEstimate(
            flops=16 * bands * patterns * columns * total * 2 * keep * 2 * keep,
            bytes_accessed=6 * bands * patterns * keep * columns * 2 * keep,
            transcendentals=0,
        ),
        name="final_x",
    )(*operands)


def permute(array, axis, step):
    return lax.ppermute(array, axis, [(i, i ^ step) for i in range(lax.axis_size(axis))])


def gather_chips(block):
    return [block] + [permute(block, "band", step) for step in range(2, lax.axis_size("band"), 2)]


def gather_cores(blocks):
    others = [permute(block, "band", 1) for block in blocks]
    return [block for pair in zip(blocks, others) for block in pair]


def cut(bands):
    sizes = [2] * ((bands - 1) // 2)
    sizes += [1] * (bands - sum(sizes))
    return [(sum(sizes[:index]), size) for index, size in enumerate(sizes)]


def halves(bands):
    middle = (bands + 1) // 2
    return [(0, middle), (middle, bands - middle)] if bands > 1 else [(0, bands)]


def holder(groups, first):
    for index, (start, count) in enumerate(groups):
        if start <= first < start + count:
            return index, first - start


def per_device(orbitals, potential_slots, pattern_owner, retained, band_energy):
    bands, local_planes, length, _ = orbitals.shape
    keep = retained.shape[1]
    patterns = pattern_owner.shape[0]
    parts = lax.axis_size("plane")
    rank = lax.axis_index("plane")
    columns = keep // parts

    ends = [max(1, local_planes // 8), max(2, local_planes * 3 // 8), local_planes]
    chunks = [
        (start, end - start, math.gcd(start, end - start)) for start, end in zip([0] + ends, ends)
    ]
    band_rank = lax.axis_index("band")
    sources = rank ^ jnp.arange(parts, dtype=jnp.int32)
    blocks = [
        lax.slice_in_dim(potential_slots[0], start, start + planes, axis=1)
        for start, planes, _ in chunks
    ]
    potentials = [(gather_cores(gather_chips(blocks[0])), band_rank ^ pattern_owner)]
    potentials += [([lax.all_gather(block, "band")], pattern_owner) for block in blocks[1:]]

    position = jnp.arange(length, dtype=jnp.int32)
    wz = right_table(retained[2], position, length)
    ty = left_table(retained[1], position, length)
    plane_order = jnp.concatenate(
        [
            (sources[:, None] * local_planes + start + jnp.arange(planes, dtype=jnp.int32)).reshape(-1)
            for start, planes, _ in chunks
        ]
    )
    tx = left_table(retained[0], plane_order, length)
    ky_local = lax.dynamic_slice_in_dim(retained[1], rank * columns, columns)
    kz = signed_square(retained[2], length)
    kinetic = kinetic_coef * (
        signed_square(retained[0], length)[:, None] + jnp.concatenate([kz, kz])[None, :]
    )
    ky = kinetic_coef * signed_square(ky_local, length)

    def run(chunk, first, count):
        start, planes, step_planes = chunks[chunk]
        slots, source = potentials[chunk]
        made = forward(
            orbitals, slots, source, sources, wz, ty, start, planes, step_planes,
            first, count, keep, patterns
        )
        return [made[0]] + [permute(made[s], "plane", s) for s in range(1, parts)]

    groups = [halves(bands)] * (len(chunks) - 1) + [cut(bands)]
    received = [
        [run(chunk, first, count) for first, count in groups[chunk]] for chunk in range(len(chunks))
    ]
    out = None
    for first, count in groups[-1]:
        places = [holder(chunk_groups, first) for chunk_groups in groups]
        out = final(
            [received[chunk][index] for chunk, (index, _) in enumerate(places)],
            [planes for _, planes, _ in chunks],
            [offset for _, offset in places],
            first, count, out, ky, band_energy, tx, kinetic, patterns, keep, bands,
        )
    return out.reshape(bands, patterns, keep, columns, 2 * keep)


def solution(mesh):
    in_specs = (
        P("band", "plane", None, None),
        P("band", None, "plane", None, None),
        P(),
        P(),
        P("band"),
    )
    out_specs = P("band", None, None, "plane", None)
    return jax.shard_map(
        per_device, mesh=mesh, in_specs=in_specs, out_specs=out_specs, check_vma=False
    )
```

```python
import functools
import math

import jax
import jax.numpy as jnp
from jax import lax
from jax.experimental import pallas as pl
from jax.experimental.pallas import tpu as pltpu
from jax.sharding import PartitionSpec as P

kinetic_coef = 0.5 * (2.0 * math.pi / 64.0) ** 2
code_top = 32700.0
code_steps = 256.0 / math.log(2.0)
vmem_limit = 56 * 1024 * 1024
f32 = jnp.float32
bf16 = jnp.bfloat16


def angle_table(frequency, position, length):
    phase_index = position[:, None] * frequency[None, :] % length
    angles = phase_index.astype(f32) * (2.0 * math.pi / length)
    norm_factor = 1.0 / math.sqrt(length)
    return jnp.cos(angles) * norm_factor, -jnp.sin(angles) * norm_factor


def signed_square(frequency, length):
    signed = jnp.where(frequency < length // 2, frequency, frequency - length).astype(f32)
    return signed * signed


def split_table(value):
    high = lax.reduce_precision(value, 8, 7)
    return high.astype(bf16), (value - high).astype(bf16)


def split_pair(value):
    high = value.astype(bf16)
    low = (value - high.astype(f32)).astype(bf16)
    return high, low


def left_table(frequency, position, length):
    cos, sin = angle_table(frequency, position, length)
    high, low = split_table(jnp.concatenate([cos, sin], axis=1).T)
    top = jnp.concatenate([high, high], axis=1)
    bottom = jnp.concatenate([low, jnp.zeros_like(low)], axis=1)
    return jnp.concatenate([top, bottom], axis=0)


def right_table(frequency, position, length):
    cos, sin = angle_table(frequency, position, length)
    table = jnp.concatenate(
        [jnp.concatenate([cos, sin], axis=1), jnp.concatenate([-sin, cos], axis=1)], axis=0
    )
    return jnp.concatenate(split_table(table), axis=1)


def left_dot(table, planes, keep):
    stacked = jnp.concatenate(
        [jnp.concatenate(split_pair(plane), axis=0) for plane in planes], axis=1
    )
    sums = jnp.dot(table, stacked, preferred_element_type=f32)
    half = 2 * keep
    sums = sums[:half] + sums[half:]
    lane = lax.broadcasted_iota(jnp.int32, (keep, half), 1)
    results = []
    for index in range(len(planes)):
        part = sums[:, index * half : (index + 1) * half]
        turned = pltpu.roll(part[keep:], keep, 1)
        results.append(part[:keep] + jnp.where(lane < keep, -turned, turned))
    return results


def pack_words(low, high):
    return (high << 16) | (low & 0xFFFF)


def unpack_words(words):
    return [((words << 16) >> 16).astype(f32), (words >> 16).astype(f32)]


def scale_rows(bands, patterns):
    return pl.cdiv(bands * (patterns // 2), 8) * 8


def forward_kernel(
    slots, planes_total, step_planes, keep, columns, patterns, parts,
    source_ref, target_ref, orbital_ref, wz_ref, ty_ref, *rest
):
    potential_refs = rest[:slots]
    out_refs = rest[slots : slots + parts]
    potential, held, semaphore = rest[slots + parts :]
    band, step = pl.program_id(0), pl.program_id(1)

    @pl.when((band == 0) & (step == 0))
    def _():
        def fetch(block, pattern):
            return pltpu.make_async_copy(block, potential.at[pattern], semaphore.at[pattern])

        gathered = slots == 1
        for pattern in range(patterns):
            if gathered:
                fetch(potential_refs[0].at[source_ref[pattern]], pattern).start()
            for slot in range(0 if gathered else slots):

                @pl.when(source_ref[pattern] == slot)
                def _():
                    fetch(potential_refs[slot], pattern).start()

        for pattern in range(patterns):
            fetch(potential_refs[0].at[0] if gathered else potential_refs[0], pattern).wait()

    def one_plane(index, carry):
        at = step * step_planes + index
        orbital = orbital_ref[0, index].astype(f32)
        highs, lows = [], []
        for pattern in range(patterns):
            split = [
                split_pair(orbital * potential[pattern, part, at].astype(f32)) for part in range(2)
            ]
            highs.append(jnp.concatenate([split[0][0], split[1][0]], axis=1))
            lows.append(jnp.concatenate([split[0][1], split[1][1]], axis=1))
        half = 2 * keep
        high_sum = jnp.dot(
            jnp.concatenate(highs, axis=0), wz_ref[...], preferred_element_type=f32
        )
        low_sum = jnp.dot(
            jnp.concatenate(lows, axis=0), wz_ref[:, :half], preferred_element_type=f32
        )
        along_z = high_sum[:, :half] + high_sum[:, half:] + low_sum
        length = orbital.shape[0]
        for pair in range(patterns // 2):
            first = 2 * pair
            results = left_dot(
                ty_ref[...],
                [along_z[p * length : (p + 1) * length] for p in (first, first + 1)],
                keep,
            )
            for offset, result in enumerate(results):
                for part in range(parts):
                    held[first + offset, at, part] = result[part * columns : (part + 1) * columns]
        return carry

    lax.fori_loop(0, step_planes, one_plane, 0, unroll=math.gcd(step_planes, 4))

    @pl.when(step == pl.num_programs(1) - 1)
    def _():
        rows = planes_total * columns
        pairs = patterns // 2
        start = pl.multiple_of(band * (pairs * rows), 8)
        for shift in range(parts):
            target = target_ref[shift]
            out_ref = out_refs[shift].at[pl.ds(start, pairs * rows), :]
            for pair in range(pairs):
                inverse, codes = [], []
                for pattern in (2 * pair, 2 * pair + 1):
                    top = jnp.zeros((columns, 2 * keep), f32)
                    for at in range(planes_total):
                        top = jnp.maximum(top, jnp.abs(held[pattern, at, target]))
                    top = jnp.max(top, axis=0, keepdims=True)
                    code = jnp.ceil(
                        jnp.log(jnp.maximum(top, 1e-30) * (1.0 / code_top)) * code_steps
                    )
                    inverse.append(jnp.exp(code * (-1.0 / code_steps)))
                    codes.append(code.astype(jnp.int32))
                scale_row = pl.num_programs(0) * (pairs * rows) + band * pairs + pair
                out_refs[shift][pl.ds(scale_row, 1), :] = pack_words(*codes)
                for at in range(planes_total):
                    low, high = [
                        jnp.round(held[2 * pair + which, at, target] * inverse[which]).astype(
                            jnp.int32
                        )
                        for which in range(2)
                    ]
                    row = pair * rows + at * columns
                    out_ref[row : row + columns, :] = pack_words(low, high)


def forward(
    orbitals, potentials, source, targets, wz, ty, first_plane, planes, step_planes, first_band,
    bands, keep, patterns
):
    parts = targets.shape[0]
    columns = keep // parts
    length = orbitals.shape[2]
    slots = len(potentials)
    rows = bands * (patterns // 2) * planes * columns + scale_rows(bands, patterns)
    kernel = functools.partial(
        forward_kernel, slots, planes, step_planes, keep, columns, patterns, parts
    )
    whole = pl.BlockSpec(memory_space=pl.ANY)
    fixed = lambda array: pl.BlockSpec(array.shape, lambda b, g, *_: (0,) * array.ndim)
    flops = 16 * bands * planes * patterns * length * length * 2 * keep
    return pl.pallas_call(
        kernel,
        grid_spec=pltpu.PrefetchScalarGridSpec(
            num_scalar_prefetch=2,
            grid=(bands, planes // step_planes),
            in_specs=[
                pl.BlockSpec(
                    (1, step_planes, length, length),
                    lambda b, g, *_: (b + first_band, g + first_plane // step_planes, 0, 0),
                ),
                fixed(wz),
                fixed(ty),
            ]
            + [whole] * slots,
            out_specs=[pl.BlockSpec((rows, 2 * keep), lambda b, g, *_: (0, 0))] * parts,
            scratch_shapes=[
                pltpu.VMEM((patterns, 2, planes, length, length), bf16),
                pltpu.VMEM((patterns, planes, parts, columns, 2 * keep), f32),
                pltpu.SemaphoreType.DMA((patterns,)),
            ],
        ),
        out_shape=[jax.ShapeDtypeStruct((rows, 2 * keep), jnp.int32)] * parts,
        compiler_params=pltpu.CompilerParams(
            dimension_semantics=("arbitrary", "arbitrary"), vmem_limit_bytes=vmem_limit
        ),
        cost_estimate=pl.CostEstimate(
            flops=flops, bytes_accessed=2 * bands * planes * length * length, transcendentals=0
        ),
        name="forward_zy",
    )(source, targets, orbitals, wz, ty, *potentials)


def final_kernel(
    plane_counts, band_offsets, first_band, keep, columns, patterns, parts, chained,
    ky_ref, energy_ref, tx_ref, kinetic_ref, *rest
):
    count = len(plane_counts) * parts
    chunk_refs, scale_refs = rest[:count], rest[count : 2 * count]
    out_ref, wide = rest[2 * count + chained :]
    energy = energy_ref[pl.program_id(0) + first_band]
    total = parts * sum(plane_counts)
    for pair in range(patterns // 2):
        base = 0
        for chunk, planes in enumerate(plane_counts):
            rows = planes * columns
            for shift in range(parts):
                place = chunk * parts + shift
                scale_row = (pl.program_id(0) + band_offsets[chunk]) * (patterns // 2) + pair
                codes = unpack_words(scale_refs[place][pl.ds(scale_row, 1), :])
                values = unpack_words(chunk_refs[place][pair * rows : (pair + 1) * rows, :])
                for which in range(2):
                    scale = jnp.exp(codes[which] * (1.0 / code_steps))
                    wide[which, base : base + rows, :] = values[which] * scale
                base += rows

        def two_columns(index, carry):
            for which in range(2):
                column = [2 * index, 2 * index + 1]
                results = left_dot(
                    tx_ref[...],
                    [wide[which, pl.ds(j, total, stride=columns), :] for j in column],
                    keep,
                )
                for j, result in zip(column, results):
                    kinetic = kinetic_ref[...] + ky_ref[j]
                    out_ref[0, 2 * pair + which, pl.ds(j, keep, stride=columns), :] = (
                        result * (1.0 / (1.0 + kinetic / energy))
                    )
            return carry

        lax.fori_loop(0, columns // 2, two_columns, 0, unroll=math.gcd(columns // 2, 4))


def final(
    chunks, plane_counts, band_offsets, group_bands, first_band, bands, held_out, ky, energy, tx,
    kinetic, patterns, keep, all_bands
):
    parts = len(chunks[0])
    columns = keep // parts
    total = parts * sum(plane_counts)
    chained = 0 if held_out is None else 1
    kernel = functools.partial(
        final_kernel, plane_counts, band_offsets, first_band, keep, columns, patterns, parts, chained
    )
    fixed = lambda array: pl.BlockSpec(array.shape, lambda b, *_: (0,) * array.ndim)
    chunk_specs, scale_specs = [], []
    for arrays, offset, planes, held_bands in zip(chunks, band_offsets, plane_counts, group_bands):
        rows = (patterns // 2) * planes * columns
        scales = scale_rows(held_bands, patterns)
        place = held_bands * rows // scales
        chunk_specs += [
            pl.BlockSpec((rows, 2 * keep), lambda b, *_, o=offset: (b + o, 0))
        ] * parts
        scale_specs += [
            pl.BlockSpec((scales, 2 * keep), lambda b, *_, at=place: (at, 0))
        ] * parts
    flat = [array for arrays in chunks for array in arrays]
    out_block = (1, patterns, keep * columns, 2 * keep)
    operands = [ky, energy, tx, kinetic] + flat + flat
    if chained:
        operands.append(held_out)
    return pl.pallas_call(
        kernel,
        grid_spec=pltpu.PrefetchScalarGridSpec(
            num_scalar_prefetch=2,
            grid=(bands,),
            in_specs=[fixed(tx), fixed(kinetic)]
            + chunk_specs
            + scale_specs
            + [pl.BlockSpec(memory_space=pl.ANY)] * chained,
            out_specs=pl.BlockSpec(out_block, lambda b, *_: (b + first_band, 0, 0, 0)),
            scratch_shapes=[pltpu.VMEM((2, total * columns, 2 * keep), f32)],
        ),
        out_shape=jax.ShapeDtypeStruct((all_bands,) + out_block[1:], f32),
        input_output_aliases={len(operands) - 1: 0} if chained else {},
        compiler_params=pltpu.CompilerParams(
            dimension_semantics=("arbitrary",), vmem_limit_bytes=vmem_limit
        ),
        cost_estimate=pl.CostEstimate(
            flops=16 * bands * patterns * columns * total * 2 * keep * 2 * keep,
            bytes_accessed=6 * bands * patterns * keep * columns * 2 * keep,
            transcendentals=0,
        ),
        name="final_x",
    )(*operands)


def permute(array, axis, step):
    return lax.ppermute(array, axis, [(i, i ^ step) for i in range(lax.axis_size(axis))])


def after(arrays, earlier):
    return lax.optimization_barrier((arrays, earlier))[0]


def gather_chips(block):
    return [block] + [permute(block, "band", step) for step in range(2, lax.axis_size("band"), 2)]


def gather_cores(blocks):
    others = [permute(block, "band", 1) for block in blocks]
    return [block for pair in zip(blocks, others) for block in pair]


def cut(bands):
    sizes = [2] * ((bands - 1) // 2)
    sizes += [1] * (bands - sum(sizes))
    return [(sum(sizes[:index]), size) for index, size in enumerate(sizes)]


def halves(bands):
    middle = (bands + 1) // 2
    return [(0, middle), (middle, bands - middle)] if bands > 1 else [(0, bands)]


def holder(groups, first):
    for index, (start, count) in enumerate(groups):
        if start <= first < start + count:
            return index, first - start


def per_device(orbitals, potential_slots, pattern_owner, retained, band_energy):
    bands, local_planes, length, _ = orbitals.shape
    keep = retained.shape[1]
    patterns = pattern_owner.shape[0]
    parts = lax.axis_size("plane")
    rank = lax.axis_index("plane")
    columns = keep // parts

    ends = [max(1, local_planes // 8), max(2, local_planes * 3 // 8), local_planes]
    chunks = [
        (start, end - start, math.gcd(start, end - start)) for start, end in zip([0] + ends, ends)
    ]
    groups = [halves(bands), halves(bands), cut(bands)]
    band_rank = lax.axis_index("band")
    steps = [0] + list(range(parts - 1, 0, -1))
    sources = rank ^ jnp.array(steps, dtype=jnp.int32)
    flipped = band_rank ^ pattern_owner
    blocks = [
        lax.slice_in_dim(potential_slots[0], start, start + planes, axis=1)
        for start, planes, _ in chunks
    ]
    position = jnp.arange(length, dtype=jnp.int32)
    wz = right_table(retained[2], position, length)
    ty = left_table(retained[1], position, length)

    chips = gather_chips(blocks[0])
    ready = after(chips, (wz, ty, flipped, sources))
    slots = [(gather_cores(ready), flipped)]
    slots += [
        ([lax.all_gather(after(block, (chips, wz, ty)), "band")], pattern_owner) for block in blocks[1:]
    ]

    def run(chunk, first, count):
        start, planes, step_planes = chunks[chunk]
        return forward(
            orbitals, *slots[chunk], sources, wz, ty, start, planes, step_planes,
            first, count, keep, patterns
        )

    def spread(blocks):
        return [blocks[0]] + [permute(*each) for each in zip(blocks[1:], ["plane"] * parts, steps[1:])]

    made = [[run(chunk, *group) for group in groups[chunk]] for chunk in range(len(chunks))]
    received = [[spread(blocks) for blocks in chunk_made] for chunk_made in made]

    late = after(retained, made[0])
    plane_order = jnp.concatenate(
        [
            (sources[:, None] * local_planes + start + jnp.arange(planes, dtype=jnp.int32)).reshape(-1)
            for start, planes, _ in chunks
        ]
    )
    tx = left_table(late[0], plane_order, length)
    ky_local = lax.dynamic_slice_in_dim(late[1], rank * columns, columns)
    kz = signed_square(late[2], length)
    kinetic = kinetic_coef * (
        signed_square(late[0], length)[:, None] + jnp.concatenate([kz, kz])[None, :]
    )
    ky = kinetic_coef * signed_square(ky_local, length)

    out = None
    for first, count in groups[-1]:
        places = [holder(chunk_groups, first) for chunk_groups in groups]
        out = final(
            [received[chunk][index] for chunk, (index, _) in enumerate(places)],
            [planes for _, planes, _ in chunks],
            [offset for _, offset in places],
            [groups[chunk][index][1] for chunk, (index, _) in enumerate(places)],
            first, count, out, ky, band_energy, tx, kinetic, patterns, keep, bands,
        )
    return out.reshape(bands, patterns, keep, columns, 2 * keep)


def solution(mesh):
    in_specs = (
        P("band", "plane", None, None),
        P("band", None, "plane", None, None),
        P(),
        P(),
        P("band"),
    )
    out_specs = P("band", None, None, "plane", None)
    return jax.shard_map(
        per_device, mesh=mesh, in_specs=in_specs, out_specs=out_specs, check_vma=False
    )
```

```python
import functools
import math

import jax
import jax.numpy as jnp
from jax import lax
from jax.experimental import pallas as pl
from jax.experimental.pallas import tpu as pltpu
from jax.sharding import PartitionSpec as P

kinetic_coef = 0.5 * (2.0 * math.pi / 64.0) ** 2
code_top = 32700.0
code_steps = 256.0 / math.log(2.0)
vmem_limit = 56 * 1024 * 1024
f32 = jnp.float32
bf16 = jnp.bfloat16


def angle_table(frequency, position, length):
    phase_index = position[:, None] * frequency[None, :] % length
    angles = phase_index.astype(f32) * (2.0 * math.pi / length)
    norm_factor = 1.0 / math.sqrt(length)
    return jnp.cos(angles) * norm_factor, -jnp.sin(angles) * norm_factor


def signed_square(frequency, length):
    signed = jnp.where(frequency < length // 2, frequency, frequency - length).astype(f32)
    return signed * signed


def split_table(value):
    high = lax.reduce_precision(value, 8, 7)
    return high.astype(bf16), (value - high).astype(bf16)


def split_pair(value):
    high = value.astype(bf16)
    low = (value - high.astype(f32)).astype(bf16)
    return high, low


def left_table(frequency, position, length):
    cos, sin = angle_table(frequency, position, length)
    high, low = split_table(jnp.concatenate([cos, sin], axis=1).T)
    top = jnp.concatenate([high, high], axis=1)
    bottom = jnp.concatenate([low, jnp.zeros_like(low)], axis=1)
    return jnp.concatenate([top, bottom], axis=0)


def right_table(frequency, position, length):
    cos, sin = angle_table(frequency, position, length)
    table = jnp.concatenate(
        [jnp.concatenate([cos, sin], axis=1), jnp.concatenate([-sin, cos], axis=1)], axis=0
    )
    return jnp.concatenate(split_table(table), axis=1)


def left_dot(table, planes, keep):
    stacked = jnp.concatenate(
        [jnp.concatenate(split_pair(plane), axis=0) for plane in planes], axis=1
    )
    sums = jnp.dot(table, stacked, preferred_element_type=f32)
    half = 2 * keep
    sums = sums[:half] + sums[half:]
    lane = lax.broadcasted_iota(jnp.int32, (keep, half), 1)
    results = []
    for index in range(len(planes)):
        part = sums[:, index * half : (index + 1) * half]
        turned = pltpu.roll(part[keep:], keep, 1)
        results.append(part[:keep] + jnp.where(lane < keep, -turned, turned))
    return results


def pack_words(low, high):
    return (high << 16) | (low & 0xFFFF)


def unpack_words(words):
    return [((words << 16) >> 16).astype(f32), (words >> 16).astype(f32)]


def scale_rows(bands, patterns):
    return pl.cdiv(bands * (patterns // 2), 8) * 8


def forward_kernel(
    slots, planes_total, step_planes, keep, columns, patterns, parts,
    source_ref, target_ref, orbital_ref, wz_ref, ty_ref, *rest
):
    potential_refs = rest[:slots]
    out_refs = rest[slots : slots + parts]
    potential, held, semaphore = rest[slots + parts :]
    band, step = pl.program_id(0), pl.program_id(1)

    @pl.when((band == 0) & (step == 0))
    def _():
        def fetch(block, pattern):
            return pltpu.make_async_copy(block, potential.at[pattern], semaphore.at[pattern])

        gathered = slots == 1
        for pattern in range(patterns):
            if gathered:
                fetch(potential_refs[0].at[source_ref[pattern]], pattern).start()
            for slot in range(0 if gathered else slots):

                @pl.when(source_ref[pattern] == slot)
                def _():
                    fetch(potential_refs[slot], pattern).start()

        for pattern in range(patterns):
            fetch(potential_refs[0].at[0] if gathered else potential_refs[0], pattern).wait()

    def one_plane(index, carry):
        at = step * step_planes + index
        orbital = orbital_ref[0, index].astype(f32)
        highs, lows = [], []
        for pattern in range(patterns):
            split = [
                split_pair(orbital * potential[pattern, part, at].astype(f32)) for part in range(2)
            ]
            highs.append(jnp.concatenate([split[0][0], split[1][0]], axis=1))
            lows.append(jnp.concatenate([split[0][1], split[1][1]], axis=1))
        half = 2 * keep
        high_sum = jnp.dot(
            jnp.concatenate(highs, axis=0), wz_ref[...], preferred_element_type=f32
        )
        low_sum = jnp.dot(
            jnp.concatenate(lows, axis=0), wz_ref[:, :half], preferred_element_type=f32
        )
        along_z = high_sum[:, :half] + high_sum[:, half:] + low_sum
        length = orbital.shape[0]
        for pair in range(patterns // 2):
            first = 2 * pair
            results = left_dot(
                ty_ref[...],
                [along_z[p * length : (p + 1) * length] for p in (first, first + 1)],
                keep,
            )
            for offset, result in enumerate(results):
                for part in range(parts):
                    held[first + offset, at, part] = result[part * columns : (part + 1) * columns]
        return carry

    lax.fori_loop(0, step_planes, one_plane, 0, unroll=math.gcd(step_planes, 4))

    @pl.when(step == pl.num_programs(1) - 1)
    def _():
        rows = planes_total * columns
        pairs = patterns // 2
        start = pl.multiple_of(band * (pairs * rows), 8)
        for shift in range(parts):
            target = target_ref[shift]
            out_ref = out_refs[shift].at[pl.ds(start, pairs * rows), :]
            for pair in range(pairs):
                inverse, codes = [], []
                for pattern in (2 * pair, 2 * pair + 1):
                    top = jnp.zeros((columns, 2 * keep), f32)
                    for at in range(planes_total):
                        top = jnp.maximum(top, jnp.abs(held[pattern, at, target]))
                    top = jnp.max(top, axis=0, keepdims=True)
                    code = jnp.ceil(
                        jnp.log(jnp.maximum(top, 1e-30) * (1.0 / code_top)) * code_steps
                    )
                    inverse.append(jnp.exp(code * (-1.0 / code_steps)))
                    codes.append(code.astype(jnp.int32))
                scale_row = pl.num_programs(0) * (pairs * rows) + band * pairs + pair
                out_refs[shift][pl.ds(scale_row, 1), :] = pack_words(*codes)
                for at in range(planes_total):
                    low, high = [
                        jnp.round(held[2 * pair + which, at, target] * inverse[which]).astype(
                            jnp.int32
                        )
                        for which in range(2)
                    ]
                    row = pair * rows + at * columns
                    out_ref[row : row + columns, :] = pack_words(low, high)


def forward(
    orbitals, potentials, source, targets, wz, ty, first_plane, planes, step_planes, first_band,
    bands, keep, patterns
):
    parts = targets.shape[0]
    columns = keep // parts
    length = orbitals.shape[2]
    slots = len(potentials)
    rows = bands * (patterns // 2) * planes * columns + scale_rows(bands, patterns)
    kernel = functools.partial(
        forward_kernel, slots, planes, step_planes, keep, columns, patterns, parts
    )
    whole = pl.BlockSpec(memory_space=pl.ANY)
    fixed = lambda array: pl.BlockSpec(array.shape, lambda b, g, *_: (0,) * array.ndim)
    flops = 16 * bands * planes * patterns * length * length * 2 * keep
    return pl.pallas_call(
        kernel,
        grid_spec=pltpu.PrefetchScalarGridSpec(
            num_scalar_prefetch=2,
            grid=(bands, planes // step_planes),
            in_specs=[
                pl.BlockSpec(
                    (1, step_planes, length, length),
                    lambda b, g, *_: (b + first_band, g + first_plane // step_planes, 0, 0),
                ),
                fixed(wz),
                fixed(ty),
            ]
            + [whole] * slots,
            out_specs=[pl.BlockSpec((rows, 2 * keep), lambda b, g, *_: (0, 0))] * parts,
            scratch_shapes=[
                pltpu.VMEM((patterns, 2, planes, length, length), bf16),
                pltpu.VMEM((patterns, planes, parts, columns, 2 * keep), f32),
                pltpu.SemaphoreType.DMA((patterns,)),
            ],
        ),
        out_shape=[jax.ShapeDtypeStruct((rows, 2 * keep), jnp.int32)] * parts,
        compiler_params=pltpu.CompilerParams(
            dimension_semantics=("arbitrary", "arbitrary"), vmem_limit_bytes=vmem_limit
        ),
        cost_estimate=pl.CostEstimate(
            flops=flops, bytes_accessed=2 * bands * planes * length * length, transcendentals=0
        ),
        name="forward_zy",
    )(source, targets, orbitals, wz, ty, *potentials)


def final_kernel(
    plane_counts, band_offsets, first_band, keep, columns, patterns, parts, chained,
    ky_ref, energy_ref, tx_ref, kinetic_ref, *rest
):
    count = len(plane_counts) * parts
    chunk_refs, scale_refs = rest[:count], rest[count : 2 * count]
    out_ref, wide = rest[2 * count + chained :]
    energy = energy_ref[pl.program_id(0) + first_band]
    total = parts * sum(plane_counts)
    for pair in range(patterns // 2):
        base = 0
        for chunk, planes in enumerate(plane_counts):
            rows = planes * columns
            for shift in range(parts):
                place = chunk * parts + shift
                scale_row = (pl.program_id(0) + band_offsets[chunk]) * (patterns // 2) + pair
                codes = unpack_words(scale_refs[place][pl.ds(scale_row, 1), :])
                values = unpack_words(chunk_refs[place][pair * rows : (pair + 1) * rows, :])
                for which in range(2):
                    scale = jnp.exp(codes[which] * (1.0 / code_steps))
                    wide[which, base : base + rows, :] = values[which] * scale
                base += rows

        def two_columns(index, carry):
            for which in range(2):
                column = [2 * index, 2 * index + 1]
                results = left_dot(
                    tx_ref[...],
                    [wide[which, pl.ds(j, total, stride=columns), :] for j in column],
                    keep,
                )
                for j, result in zip(column, results):
                    kinetic = kinetic_ref[...] + ky_ref[j]
                    out_ref[0, 2 * pair + which, pl.ds(j, keep, stride=columns), :] = (
                        result * (1.0 / (1.0 + kinetic / energy))
                    )
            return carry

        lax.fori_loop(0, columns // 2, two_columns, 0, unroll=math.gcd(columns // 2, 8))


def final(
    chunks, plane_counts, band_offsets, group_bands, first_band, bands, held_out, ky, energy, tx,
    kinetic, patterns, keep, all_bands
):
    parts = len(chunks[0])
    columns = keep // parts
    total = parts * sum(plane_counts)
    chained = 0 if held_out is None else 1
    kernel = functools.partial(
        final_kernel, plane_counts, band_offsets, first_band, keep, columns, patterns, parts, chained
    )
    fixed = lambda array: pl.BlockSpec(array.shape, lambda b, *_: (0,) * array.ndim)
    chunk_specs, scale_specs = [], []
    for arrays, offset, planes, held_bands in zip(chunks, band_offsets, plane_counts, group_bands):
        rows = (patterns // 2) * planes * columns
        scales = scale_rows(held_bands, patterns)
        place = held_bands * rows // scales
        chunk_specs += [
            pl.BlockSpec((rows, 2 * keep), lambda b, *_, o=offset: (b + o, 0))
        ] * parts
        scale_specs += [
            pl.BlockSpec((scales, 2 * keep), lambda b, *_, at=place: (at, 0))
        ] * parts
    flat = [array for arrays in chunks for array in arrays]
    out_block = (1, patterns, keep * columns, 2 * keep)
    operands = [ky, energy, tx, kinetic] + flat + flat
    if chained:
        operands.append(held_out)
    return pl.pallas_call(
        kernel,
        grid_spec=pltpu.PrefetchScalarGridSpec(
            num_scalar_prefetch=2,
            grid=(bands,),
            in_specs=[fixed(tx), fixed(kinetic)]
            + chunk_specs
            + scale_specs
            + [pl.BlockSpec(memory_space=pl.ANY)] * chained,
            out_specs=pl.BlockSpec(out_block, lambda b, *_: (b + first_band, 0, 0, 0)),
            scratch_shapes=[pltpu.VMEM((2, total * columns, 2 * keep), f32)],
        ),
        out_shape=jax.ShapeDtypeStruct((all_bands,) + out_block[1:], f32),
        input_output_aliases={len(operands) - 1: 0} if chained else {},
        compiler_params=pltpu.CompilerParams(
            dimension_semantics=("arbitrary",), vmem_limit_bytes=vmem_limit
        ),
        cost_estimate=pl.CostEstimate(
            flops=16 * bands * patterns * columns * total * 2 * keep * 2 * keep,
            bytes_accessed=6 * bands * patterns * keep * columns * 2 * keep,
            transcendentals=0,
        ),
        name="final_x",
    )(*operands)


def permute(array, axis, step):
    return lax.ppermute(array, axis, [(i, i ^ step) for i in range(lax.axis_size(axis))])


def after(arrays, earlier):
    return lax.optimization_barrier((arrays, earlier))[0]


def gather_chips(block):
    return [block] + [permute(block, "band", step) for step in range(2, lax.axis_size("band"), 2)]


def gather_cores(blocks):
    others = [permute(block, "band", 1) for block in blocks]
    return [block for pair in zip(blocks, others) for block in pair]


def cut(bands):
    sizes = [2] * ((bands - 1) // 2)
    sizes += [1] * (bands - sum(sizes))
    return [(sum(sizes[:index]), size) for index, size in enumerate(sizes)]


def halves(bands):
    middle = (bands + 1) // 2
    return [(0, middle), (middle, bands - middle)] if bands > 1 else [(0, bands)]


def holder(groups, first):
    for index, (start, count) in enumerate(groups):
        if start <= first < start + count:
            return index, first - start


def per_device(orbitals, potential_slots, pattern_owner, retained, band_energy):
    bands, local_planes, length, _ = orbitals.shape
    keep = retained.shape[1]
    patterns = pattern_owner.shape[0]
    parts = lax.axis_size("plane")
    rank = lax.axis_index("plane")
    columns = keep // parts

    ends = [max(1, local_planes // 8), max(2, local_planes * 3 // 8), local_planes]
    chunks = [
        (start, end - start, math.gcd(start, end - start)) for start, end in zip([0] + ends, ends)
    ]
    groups = [halves(bands), halves(bands), cut(bands)]
    band_rank = lax.axis_index("band")
    steps = [0] + list(range(parts - 1, 0, -1))
    sources = rank ^ jnp.array(steps, dtype=jnp.int32)
    flipped = band_rank ^ pattern_owner
    def planes_of(slot, chunk):
        start, planes, _ = chunks[chunk]
        return lax.slice_in_dim(slot, start, start + planes, axis=1)

    position = jnp.arange(length, dtype=jnp.int32)
    wz = right_table(retained[2], position, length)
    ty = left_table(retained[1], position, length)

    own = potential_slots[0]
    tables = (wz, ty, flipped, sources)
    chips = gather_chips(planes_of(own, 0))
    slots = [(gather_cores(after(chips, tables)), flipped)]
    next_block = after(planes_of(own, 1), (chips, tables))
    slots.append(([lax.all_gather(next_block, "band")], pattern_owner))

    def run(chunk, first, count):
        start, planes, step_planes = chunks[chunk]
        return forward(
            orbitals, *slots[chunk], sources, wz, ty, start, planes, step_planes,
            first, count, keep, patterns
        )

    def spread(blocks):
        return [blocks[0]] + [permute(*each) for each in zip(blocks[1:], ["plane"] * parts, steps[1:])]

    made = [[run(0, *group) for group in groups[0]]]
    last_block = planes_of(after(own, made[0]), 2)
    slots.append(([lax.all_gather(last_block, "band")], pattern_owner))
    made += [[run(chunk, *group) for group in groups[chunk]] for chunk in (1, 2)]
    received = [[spread(blocks) for blocks in chunk_made] for chunk_made in made]

    late = after(retained, made[0])
    plane_order = jnp.concatenate(
        [
            (sources[:, None] * local_planes + start + jnp.arange(planes, dtype=jnp.int32)).reshape(-1)
            for start, planes, _ in chunks
        ]
    )
    tx = left_table(late[0], plane_order, length)
    ky_local = lax.dynamic_slice_in_dim(late[1], rank * columns, columns)
    kz = signed_square(late[2], length)
    kinetic = kinetic_coef * (
        signed_square(late[0], length)[:, None] + jnp.concatenate([kz, kz])[None, :]
    )
    ky = kinetic_coef * signed_square(ky_local, length)

    out = None
    for first, count in groups[-1]:
        places = [holder(chunk_groups, first) for chunk_groups in groups]
        out = final(
            [received[chunk][index] for chunk, (index, _) in enumerate(places)],
            [planes for _, planes, _ in chunks],
            [offset for _, offset in places],
            [groups[chunk][index][1] for chunk, (index, _) in enumerate(places)],
            first, count, out, ky, band_energy, tx, kinetic, patterns, keep, bands,
        )
    return out.reshape(bands, patterns, keep, columns, 2 * keep)


def solution(mesh):
    in_specs = (
        P("band", "plane", None, None),
        P("band", None, "plane", None, None),
        P(),
        P(),
        P("band"),
    )
    out_specs = P("band", None, None, "plane", None)
    return jax.shard_map(
        per_device, mesh=mesh, in_specs=in_specs, out_specs=out_specs, check_vma=False
    )
```

```python
import functools
import math

import jax
import jax.numpy as jnp
from jax import lax
from jax.experimental import pallas as pl
from jax.experimental.pallas import tpu as pltpu
from jax.sharding import PartitionSpec as P

kinetic_coef = 0.5 * (2.0 * math.pi / 64.0) ** 2
code_top = 32700.0
code_steps = 256.0 / math.log(2.0)
vmem_limit = 56 * 1024 * 1024
f32 = jnp.float32
bf16 = jnp.bfloat16


def angle_table(frequency, position, length):
    phase_index = position[:, None] * frequency[None, :] % length
    angles = phase_index.astype(f32) * (2.0 * math.pi / length)
    norm_factor = 1.0 / math.sqrt(length)
    return jnp.cos(angles) * norm_factor, -jnp.sin(angles) * norm_factor


def signed_square(frequency, length):
    signed = jnp.where(frequency < length // 2, frequency, frequency - length).astype(f32)
    return signed * signed


def split_table(value):
    high = lax.reduce_precision(value, 8, 7)
    return high.astype(bf16), (value - high).astype(bf16)


def split_pair(value):
    high = value.astype(bf16)
    low = (value - high.astype(f32)).astype(bf16)
    return high, low


def left_table(frequency, position, length):
    cos, sin = angle_table(frequency, position, length)
    high, low = split_table(jnp.concatenate([cos, sin], axis=1).T)
    top = jnp.concatenate([high, high], axis=1)
    bottom = jnp.concatenate([low, jnp.zeros_like(low)], axis=1)
    return jnp.concatenate([top, bottom], axis=0)


def right_table(frequency, position, length):
    cos, sin = angle_table(frequency, position, length)
    table = jnp.concatenate(
        [jnp.concatenate([cos, sin], axis=1), jnp.concatenate([-sin, cos], axis=1)], axis=0
    )
    return jnp.concatenate(split_table(table), axis=1)


def left_dot(table, planes, keep):
    stacked = jnp.concatenate(
        [jnp.concatenate(split_pair(plane), axis=0) for plane in planes], axis=1
    )
    sums = jnp.dot(table, stacked, preferred_element_type=f32)
    half = 2 * keep
    sums = sums[:half] + sums[half:]
    lane = lax.broadcasted_iota(jnp.int32, (keep, half), 1)
    results = []
    for index in range(len(planes)):
        part = sums[:, index * half : (index + 1) * half]
        turned = pltpu.roll(part[keep:], keep, 1)
        results.append(part[:keep] + jnp.where(lane < keep, -turned, turned))
    return results


def pack_words(low, high):
    return (high << 16) | (low & 0xFFFF)


def unpack_words(words):
    return [((words << 16) >> 16).astype(f32), (words >> 16).astype(f32)]


def scale_rows(bands, patterns):
    return pl.cdiv(bands * (patterns // 2), 8) * 8


def forward_kernel(
    slots, planes_total, step_planes, keep, columns, patterns, parts,
    source_ref, target_ref, orbital_ref, wz_ref, ty_ref, *rest
):
    potential_refs = rest[:slots]
    out_refs = rest[slots : slots + parts]
    potential, held, semaphore = rest[slots + parts :]
    band, step = pl.program_id(0), pl.program_id(1)

    @pl.when((band == 0) & (step == 0))
    def _():
        def fetch(block, pattern):
            return pltpu.make_async_copy(block, potential.at[pattern], semaphore.at[pattern])

        gathered = slots == 1
        for pattern in range(patterns):
            if gathered:
                fetch(potential_refs[0].at[source_ref[pattern]], pattern).start()
            for slot in range(0 if gathered else slots):

                @pl.when(source_ref[pattern] == slot)
                def _():
                    fetch(potential_refs[slot], pattern).start()

        for pattern in range(patterns):
            fetch(potential_refs[0].at[0] if gathered else potential_refs[0], pattern).wait()

    def one_plane(index, carry):
        at = step * step_planes + index
        orbital = orbital_ref[0, index].astype(f32)
        highs, lows = [], []
        for pattern in range(patterns):
            split = [
                split_pair(orbital * potential[pattern, part, at].astype(f32)) for part in range(2)
            ]
            highs.append(jnp.concatenate([split[0][0], split[1][0]], axis=1))
            lows.append(jnp.concatenate([split[0][1], split[1][1]], axis=1))
        half = 2 * keep
        high_sum = jnp.dot(
            jnp.concatenate(highs, axis=0), wz_ref[...], preferred_element_type=f32
        )
        low_sum = jnp.dot(
            jnp.concatenate(lows, axis=0), wz_ref[:, :half], preferred_element_type=f32
        )
        along_z = high_sum[:, :half] + high_sum[:, half:] + low_sum
        length = orbital.shape[0]
        for pair in range(patterns // 2):
            first = 2 * pair
            results = left_dot(
                ty_ref[...],
                [along_z[p * length : (p + 1) * length] for p in (first, first + 1)],
                keep,
            )
            for offset, result in enumerate(results):
                for part in range(parts):
                    held[first + offset, at, part] = result[part * columns : (part + 1) * columns]
        return carry

    lax.fori_loop(0, step_planes, one_plane, 0, unroll=math.gcd(step_planes, 4))

    @pl.when(step == pl.num_programs(1) - 1)
    def _():
        rows = planes_total * columns
        pairs = patterns // 2
        start = pl.multiple_of(band * (pairs * rows), 8)
        for shift in range(parts):
            target = target_ref[shift]
            out_ref = out_refs[shift].at[pl.ds(start, pairs * rows), :]
            for pair in range(pairs):
                inverse, codes = [], []
                for pattern in (2 * pair, 2 * pair + 1):
                    top = jnp.zeros((columns, 2 * keep), f32)
                    for at in range(planes_total):
                        top = jnp.maximum(top, jnp.abs(held[pattern, at, target]))
                    top = jnp.max(top, axis=0, keepdims=True)
                    code = jnp.ceil(
                        jnp.log(jnp.maximum(top, 1e-30) * (1.0 / code_top)) * code_steps
                    )
                    inverse.append(jnp.exp(code * (-1.0 / code_steps)))
                    codes.append(code.astype(jnp.int32))
                scale_row = pl.num_programs(0) * (pairs * rows) + band * pairs + pair
                out_refs[shift][pl.ds(scale_row, 1), :] = pack_words(*codes)
                for at in range(planes_total):
                    low, high = [
                        jnp.round(held[2 * pair + which, at, target] * inverse[which]).astype(
                            jnp.int32
                        )
                        for which in range(2)
                    ]
                    row = pair * rows + at * columns
                    out_ref[row : row + columns, :] = pack_words(low, high)


def forward(
    orbitals, potentials, source, targets, wz, ty, first_plane, planes, step_planes, first_band,
    bands, keep, patterns
):
    parts = targets.shape[0]
    columns = keep // parts
    length = orbitals.shape[2]
    slots = len(potentials)
    rows = bands * (patterns // 2) * planes * columns + scale_rows(bands, patterns)
    kernel = functools.partial(
        forward_kernel, slots, planes, step_planes, keep, columns, patterns, parts
    )
    whole = pl.BlockSpec(memory_space=pl.ANY)
    fixed = lambda array: pl.BlockSpec(array.shape, lambda b, g, *_: (0,) * array.ndim)
    flops = 16 * bands * planes * patterns * length * length * 2 * keep
    return pl.pallas_call(
        kernel,
        grid_spec=pltpu.PrefetchScalarGridSpec(
            num_scalar_prefetch=2,
            grid=(bands, planes // step_planes),
            in_specs=[
                pl.BlockSpec(
                    (1, step_planes, length, length),
                    lambda b, g, *_: (b + first_band, g + first_plane // step_planes, 0, 0),
                ),
                fixed(wz),
                fixed(ty),
            ]
            + [whole] * slots,
            out_specs=[pl.BlockSpec((rows, 2 * keep), lambda b, g, *_: (0, 0))] * parts,
            scratch_shapes=[
                pltpu.VMEM((patterns, 2, planes, length, length), bf16),
                pltpu.VMEM((patterns, planes, parts, columns, 2 * keep), f32),
                pltpu.SemaphoreType.DMA((patterns,)),
            ],
        ),
        out_shape=[jax.ShapeDtypeStruct((rows, 2 * keep), jnp.int32)] * parts,
        compiler_params=pltpu.CompilerParams(
            dimension_semantics=("arbitrary", "arbitrary"), vmem_limit_bytes=vmem_limit
        ),
        cost_estimate=pl.CostEstimate(
            flops=flops, bytes_accessed=2 * bands * planes * length * length, transcendentals=0
        ),
        name="forward_zy",
    )(source, targets, orbitals, wz, ty, *potentials)


def final_kernel(
    plane_counts, band_offsets, first_band, keep, columns, patterns, parts, chained,
    ky_ref, energy_ref, tx_ref, kinetic_ref, *rest
):
    count = len(plane_counts) * parts
    chunk_refs, scale_refs = rest[:count], rest[count : 2 * count]
    out_ref, wide = rest[2 * count + chained :]
    energy = energy_ref[pl.program_id(0) + first_band]
    total = parts * sum(plane_counts)
    for pair in range(patterns // 2):
        base = 0
        for chunk, planes in enumerate(plane_counts):
            rows = planes * columns
            for shift in range(parts):
                place = chunk * parts + shift
                scale_row = (pl.program_id(0) + band_offsets[chunk]) * (patterns // 2) + pair
                codes = unpack_words(scale_refs[place][pl.ds(scale_row, 1), :])
                values = unpack_words(chunk_refs[place][pair * rows : (pair + 1) * rows, :])
                for which in range(2):
                    scale = jnp.exp(codes[which] * (1.0 / code_steps))
                    wide[which, base : base + rows, :] = values[which] * scale
                base += rows

        def two_columns(index, carry):
            for which in range(2):
                column = [2 * index, 2 * index + 1]
                results = left_dot(
                    tx_ref[...],
                    [wide[which, pl.ds(j, total, stride=columns), :] for j in column],
                    keep,
                )
                for j, result in zip(column, results):
                    kinetic = kinetic_ref[...] + ky_ref[j]
                    out_ref[0, 2 * pair + which, pl.ds(j, keep, stride=columns), :] = (
                        result * (1.0 / (1.0 + kinetic / energy))
                    )
            return carry

        lax.fori_loop(0, columns // 2, two_columns, 0, unroll=math.gcd(columns // 2, 8))


def final(
    chunks, plane_counts, band_offsets, group_bands, first_band, bands, held_out, ky, energy, tx,
    kinetic, patterns, keep, all_bands
):
    parts = len(chunks[0])
    columns = keep // parts
    total = parts * sum(plane_counts)
    chained = 0 if held_out is None else 1
    kernel = functools.partial(
        final_kernel, plane_counts, band_offsets, first_band, keep, columns, patterns, parts, chained
    )
    fixed = lambda array: pl.BlockSpec(array.shape, lambda b, *_: (0,) * array.ndim)
    chunk_specs, scale_specs = [], []
    for arrays, offset, planes, held_bands in zip(chunks, band_offsets, plane_counts, group_bands):
        rows = (patterns // 2) * planes * columns
        scales = scale_rows(held_bands, patterns)
        place = held_bands * rows // scales
        chunk_specs += [
            pl.BlockSpec((rows, 2 * keep), lambda b, *_, o=offset: (b + o, 0))
        ] * parts
        scale_specs += [
            pl.BlockSpec((scales, 2 * keep), lambda b, *_, at=place: (at, 0))
        ] * parts
    flat = [array for arrays in chunks for array in arrays]
    out_block = (1, patterns, keep * columns, 2 * keep)
    operands = [ky, energy, tx, kinetic] + flat + flat
    if chained:
        operands.append(held_out)
    return pl.pallas_call(
        kernel,
        grid_spec=pltpu.PrefetchScalarGridSpec(
            num_scalar_prefetch=2,
            grid=(bands,),
            in_specs=[fixed(tx), fixed(kinetic)]
            + chunk_specs
            + scale_specs
            + [pl.BlockSpec(memory_space=pl.ANY)] * chained,
            out_specs=pl.BlockSpec(out_block, lambda b, *_: (b + first_band, 0, 0, 0)),
            scratch_shapes=[pltpu.VMEM((2, total * columns, 2 * keep), f32)],
        ),
        out_shape=jax.ShapeDtypeStruct((all_bands,) + out_block[1:], f32),
        input_output_aliases={len(operands) - 1: 0} if chained else {},
        compiler_params=pltpu.CompilerParams(
            dimension_semantics=("arbitrary",), vmem_limit_bytes=vmem_limit
        ),
        cost_estimate=pl.CostEstimate(
            flops=16 * bands * patterns * columns * total * 2 * keep * 2 * keep,
            bytes_accessed=6 * bands * patterns * keep * columns * 2 * keep,
            transcendentals=0,
        ),
        name="final_x",
    )(*operands)


def permute(array, axis, step):
    return lax.ppermute(array, axis, [(i, i ^ step) for i in range(lax.axis_size(axis))])


def after(arrays, earlier):
    return lax.optimization_barrier((arrays, earlier))[0]


def gather_chips(block):
    return [block] + [permute(block, "band", step) for step in range(2, lax.axis_size("band"), 2)]


def gather_cores(blocks):
    others = [permute(block, "band", 1) for block in blocks]
    return [block for pair in zip(blocks, others) for block in pair]


def cut(bands):
    sizes = [2] * ((bands - 1) // 2)
    sizes += [1] * (bands - sum(sizes))
    return [(sum(sizes[:index]), size) for index, size in enumerate(sizes)]


def halves(bands):
    middle = (bands + 1) // 2
    return [(0, middle), (middle, bands - middle)] if bands > 1 else [(0, bands)]


def holder(groups, first):
    for index, (start, count) in enumerate(groups):
        if start <= first < start + count:
            return index, first - start


def per_device(orbitals, potential_slots, pattern_owner, retained, band_energy):
    bands, local_planes, length, _ = orbitals.shape
    keep = retained.shape[1]
    patterns = pattern_owner.shape[0]
    parts = lax.axis_size("plane")
    rank = lax.axis_index("plane")
    columns = keep // parts

    ends = [max(1, local_planes // 8), max(2, local_planes * 3 // 8), local_planes]
    chunks = [
        (start, end - start, math.gcd(start, end - start)) for start, end in zip([0] + ends, ends)
    ]
    groups = [halves(bands), halves(bands), cut(bands)]
    band_rank = lax.axis_index("band")
    steps = [0] + list(range(parts - 1, 0, -1))
    sources = rank ^ jnp.array(steps, dtype=jnp.int32)
    flipped = band_rank ^ pattern_owner
    def planes_of(slot, chunk):
        start, planes, _ = chunks[chunk]
        return lax.slice_in_dim(slot, start, start + planes, axis=1)

    position = jnp.arange(length, dtype=jnp.int32)
    wz = right_table(retained[2], position, length)
    ty = left_table(retained[1], position, length)

    own = potential_slots[0]
    tables = (wz, ty, flipped, sources)
    chips = gather_chips(planes_of(own, 0))
    slots = [(gather_cores(after(chips, tables)), flipped)]
    next_block = after(planes_of(own, 1), (chips, tables))
    slots.append(([lax.all_gather(next_block, "band")], pattern_owner))

    def run(chunk, first, count):
        start, planes, step_planes = chunks[chunk]
        return forward(
            orbitals, *slots[chunk], sources, wz, ty, start, planes, step_planes,
            first, count, keep, patterns
        )

    def spread(blocks):
        return [blocks[0]] + [permute(*each) for each in zip(blocks[1:], ["plane"] * parts, steps[1:])]

    made = [[run(0, *group) for group in groups[0]]]
    last_block = planes_of(after(own, made[0][0]), 2)
    slots.append(([lax.all_gather(last_block, "band")], pattern_owner))
    made += [[run(chunk, *group) for group in groups[chunk]] for chunk in (1, 2)]
    received = [[spread(blocks) for blocks in chunk_made] for chunk_made in made]

    late = after(retained, made[0])
    plane_order = jnp.concatenate(
        [
            (sources[:, None] * local_planes + start + jnp.arange(planes, dtype=jnp.int32)).reshape(-1)
            for start, planes, _ in chunks
        ]
    )
    tx = left_table(late[0], plane_order, length)
    ky_local = lax.dynamic_slice_in_dim(late[1], rank * columns, columns)
    kz = signed_square(late[2], length)
    kinetic = kinetic_coef * (
        signed_square(late[0], length)[:, None] + jnp.concatenate([kz, kz])[None, :]
    )
    ky = kinetic_coef * signed_square(ky_local, length)

    out = None
    for first, count in groups[-1]:
        places = [holder(chunk_groups, first) for chunk_groups in groups]
        out = final(
            [received[chunk][index] for chunk, (index, _) in enumerate(places)],
            [planes for _, planes, _ in chunks],
            [offset for _, offset in places],
            [groups[chunk][index][1] for chunk, (index, _) in enumerate(places)],
            first, count, out, ky, band_energy, tx, kinetic, patterns, keep, bands,
        )
    return out.reshape(bands, patterns, keep, columns, 2 * keep)


def solution(mesh):
    in_specs = (
        P("band", "plane", None, None),
        P("band", None, "plane", None, None),
        P(),
        P(),
        P("band"),
    )
    out_specs = P("band", None, None, "plane", None)
    return jax.shard_map(
        per_device, mesh=mesh, in_specs=in_specs, out_specs=out_specs, check_vma=False
    )
```
